32 devices in a mesh: groups: 2 (over x), particle: 8 (over z, y), seq: 2 (over core).
Axes of the slice: x: 2, y: 2, z: 4, core: 2. Of those that a mesh axis runs over, the one named last changes fastest.
Arguments:
- latents: float32 [16, 1024, 64], P(('groups', 'particle'), 'seq'), parts along dimension 0, may hold values from -6 to 6
- text_kv: bfloat16 [16, 2, 256, 1536], P(('groups', 'particle'), None, None, 'seq'), parts along dimension 0, may hold values from -20 to 20
- ancestors: int32 [16], P('groups'), parts along dimension 0, may hold values from 0 to 7
- order: int32 [16], P('groups'), parts along dimension 0, may hold values from 0 to 7, each once
- embed_weight: bfloat16 [64, 3072], replicated, may hold values from -0.75 to 0.75
- embed_bias: float32 [3072], replicated, may hold values from -3 to 3
- shift: float32 [6144], P('groups'), parts along dimension 0, may hold values from -3 to 3
- scale: float32 [6144], P('groups'), parts along dimension 0, may hold values from -0.9 to 0.9
- qkv_weight: bfloat16 [3072, 4608], P(None, 'seq'), may hold values from -4 to 4
- norm_gains: float32 [2, 128], replicated, may hold values from 0.5 to 2
Outputs:
- attended: bfloat16 [16, 1024, 1536], P(('groups', 'particle'), 'seq'), parts along dimension 0
The draws below stay inside these ranges and needn't reach their ends.
There are 2 independent parts, one for each index of `groups`. The reference program is written for one: setup_inputs(seed, part) draws one part's arguments, and reference() takes and returns one part's arrays. A program takes and returns all parts, laid end to end along the dimension named above; an argument that names none is the same for every part. Nothing has to cross between parts.
All inputs are finite; a program needn't handle non-finite values.
Results may differ from the reference program's by a relative error of at most 0.012.
The reference program's roundings to bfloat16 on the way (of `picked`, `text`, `normed`, `query` and `weights`) count: a program that leaves them out, or rounds other values in their place, can miss the bound.
Values may be sent and summed in bfloat16 or wider, within the bound.
A program may use at most 128 MiB of HBM per device.

```python
import math
import jax
import jax.numpy as jnp
import numpy as np
from jax import lax

D = 3072
HEADS = 12
HD = 128
CH = 64
TXT = 256
TOK = 1024
PARTICLES = 8


def draw_text_kv(key, part):
    key = jax.random.fold_in(key, 7)
    first = jax.random.fold_in(key, 0)
    shape = (PARTICLES, 2, TXT, HEADS * HD)
    values = jnp.clip(jax.random.normal(first, shape) * 1.5, -9.0, 9.0)
    return values.astype(jnp.bfloat16)


def draw_qkv_weight(key, part):
    key = jax.random.fold_in(key, 11)
    first = jax.random.fold_in(key, 0)
    values = jax.random.normal(first, (D, 3 * HEADS * HD)) * D ** (-0.5)
    return jnp.clip(values, -4.0, 4.0).astype(jnp.bfloat16)


def set_ends(result, stream_key, low, high):
    spot = [jax.random.randint(jax.random.fold_in(stream_key, axis), (), 0, length) for axis, length in enumerate(result.shape)]
    widest = result.shape.index(max(result.shape))
    neighbour = spot[:widest] + [(spot[widest] + 1) % result.shape[widest]] + spot[widest + 1:]
    return result.at[tuple(spot)].set(low).at[tuple(neighbour)].set(high)


def level_of(rng, extent, shards, least, high):
    level, own = 1.0, jax.random.fold_in(rng, 6)
    for axis_at, parts in shards:
        heights = jnp.exp(jax.random.uniform(jax.random.fold_in(own, axis_at), (parts,), jnp.float32, least / len(shards), high / len(shards)))
        level = level * jnp.repeat(heights, extent[axis_at] // parts).reshape([-1 if axis == axis_at else 1 for axis in range(len(extent))])
    return level


def rank_bounds(number_of, slope):
    weights = [(1 << 20) // math.isqrt(rank ** slope) + 1 for rank in range(1, number_of + 1)]
    width = 1 + sum(weights) // (1 << 30)
    return np.cumsum(np.array([max(1, weight // width) for weight in weights]))


def ranked_ids(rng, extent, count, skew):
    grid = rank_bounds(count, skew)
    ticket = jax.random.randint(jax.random.fold_in(rng, 1), extent, 0, int(grid[count - 1]))
    standing = jnp.searchsorted(jnp.asarray(grid, jnp.int32), ticket, side="right")
    return jax.random.permutation(jax.random.fold_in(rng, 2), count)[standing].astype(jnp.int32)


def gaussian(own_key, dims, scale, most, pieces=(), dtype=jnp.bfloat16):
    result = jax.random.normal(own_key, dims, jnp.float32) * scale
    if len(pieces) > 0:
        result = level_of(own_key, dims, pieces, -0.22, 0.18) * result
    return jnp.clip(result, min=-most, max=most).astype(dtype)


def setup_inputs(seed: int = 0, part: int = 0) -> dict:
    streams_of = jax.random.split(jax.random.key(seed), 11)
    own_keys = jax.random.split(jax.random.fold_in(streams_of[10], part), 11)
    return {
        "latents": gaussian(own_keys[0], (PARTICLES, TOK, CH), 1.0, 6.0, ((0, 8), (1, 2)), jnp.float32),
        "text_kv": draw_text_kv(jax.random.fold_in(jax.random.fold_in(streams_of[10], part), 71), part),
        "ancestors": set_ends(ranked_ids(own_keys[2], (PARTICLES,), PARTICLES, 2), jax.random.fold_in(own_keys[2], 3), 0, PARTICLES - 1).astype(jnp.int32),
        "order": jax.random.permutation(own_keys[3], PARTICLES).astype(jnp.int32),
        "embed_weight": gaussian(streams_of[4], (CH, D), CH ** -0.5, 0.75),
        "embed_bias": gaussian(streams_of[5], (D,), 0.5, 3.0, (), jnp.float32),
        "shift": gaussian(own_keys[6], (D,), 0.5, 3.0, (), jnp.float32),
        "scale": gaussian(own_keys[7], (D,), 0.3, 0.9, (), jnp.float32),
        "qkv_weight": draw_qkv_weight(jax.random.fold_in(streams_of[10], 71), part),
        "norm_gains": jnp.clip(jnp.exp(jax.random.uniform(streams_of[9], (2, HD), jnp.float32, math.log(0.5), math.log(2.0))), 0.5, 2.0),
    }


def rms_norm(values, gain):
    return values * lax.rsqrt(lax.optimization_barrier(jnp.mean(values * values, axis=-1, keepdims=True)) + 1e-06) * gain

def reference(latents, text_kv, ancestors, order, embed_weight, embed_bias, shift, scale, qkv_weight, norm_gains):
    chosen = ancestors[order].astype(jnp.int32)
    picked = jnp.take(latents, chosen, axis=0).astype(jnp.bfloat16)
    text = jnp.take(text_kv, chosen, axis=0)

    def one_particle(operands):
        lat_rows, text_rows = operands
        embedded = jnp.dot(lat_rows, embed_weight, preferred_element_type=jnp.float32) + embed_bias
        center = embedded - lax.optimization_barrier(jnp.mean(embedded, axis=-1, keepdims=True))
        spread = lax.optimization_barrier(jnp.mean(center * center, axis=-1, keepdims=True))
        normed = (center * lax.rsqrt(spread + 1e-06) * (1.0 + scale) + shift).astype(jnp.bfloat16)
        mixed = jnp.dot(normed, qkv_weight, preferred_element_type=jnp.float32).reshape(TOK, HEADS, 3, HD)
        query = rms_norm(mixed[:, :, 0], norm_gains[0]).astype(jnp.bfloat16)
        key_img = rms_norm(mixed[:, :, 1], norm_gains[1]).astype(jnp.bfloat16)
        val_img = mixed[:, :, 2].astype(jnp.bfloat16)
        text_keys = text_rows[0].reshape(TXT, HEADS, HD)
        text_vals = text_rows[1].reshape(TXT, HEADS, HD)
        keys = jnp.concatenate([text_keys, key_img], axis=0).astype(jnp.float32)
        vals = jnp.concatenate([text_vals, val_img], axis=0).astype(jnp.float32)
        scores = jnp.einsum('qhd,khd->hqk', query.astype(jnp.float32), keys) / jnp.sqrt(jnp.float32(HD))
        weights = jax.nn.softmax(scores, axis=-1).astype(jnp.bfloat16)
        output = jnp.einsum('hqk,khd->qhd', weights.astype(jnp.float32), vals)
        return output.reshape(TOK, HEADS * HD).astype(jnp.bfloat16)
    return lax.map(one_particle, (picked, text))
```

```python
import functools
import jax
import jax.numpy as jnp
from jax import lax
from jax.experimental import pallas as pl
from jax.experimental.pallas import tpu as pltpu
from jax.sharding import PartitionSpec as P

LOG2E = 1.4426950408889634
BF16 = jnp.bfloat16
F32 = jnp.float32
NT = (((1,), (1,)), ((), ()))


def rms_norm(values, gain):
    return values * lax.rsqrt(jnp.mean(values * values, axis=-1, keepdims=True) + 1e-06) * gain


def project_kernel(x0_ref, x1_ref, ew_ref, eb_ref, sh_ref, sc_ref, gain_ref, w_ref,
                   q_ref, k_ref, v_ref, normed, *, chunk, width):
    half = x0_ref.shape[0] * 2
    lanes = x0_ref.shape[1] // 2

    @pl.when(pl.program_id(0) == 0)
    def _():
        for part, x_ref in enumerate((x0_ref, x1_ref)):
            for side in range(2):
                for at in range(0, half // 2, chunk):
                    x = x_ref[at:at + chunk, side * lanes:(side + 1) * lanes]
                    emb = jnp.dot(x, ew_ref[...], preferred_element_type=F32) + eb_ref[...]
                    center = emb - jnp.mean(emb, axis=-1, keepdims=True)
                    spread = jnp.mean(center * center, axis=-1, keepdims=True)
                    res = center * lax.rsqrt(spread + 1e-06) * (1.0 + sc_ref[...]) + sh_ref[...]
                    row = part * half + side * (half // 2) + at
                    normed[row:row + chunk, :] = res.astype(BF16)

    rows = normed.shape[0]
    heads = w_ref.shape[1] // (3 * width)
    step = 256

    @pl.loop(0, rows // step)
    def _(i):
        r = pl.ds(pl.multiple_of(i * step, step), step)
        mixed = jnp.dot(normed[r, :], w_ref[...], preferred_element_type=F32)
        for h in range(heads):
            c = slice(h * width, (h + 1) * width)
            base = h * 3 * width
            q_ref[r, c] = rms_norm(mixed[:, base:base + width], gain_ref[0:1, :]).astype(BF16)
            k_ref[r, c] = rms_norm(
                mixed[:, base + width:base + 2 * width], gain_ref[1:2, :]
            ).astype(BF16)
            v_ref[r, c] = mixed[:, base + 2 * width:base + 3 * width].astype(BF16)


def project(x0, x1, embed_weight, embed_bias, shift, scale, gains, weight):
    d, cols = weight.shape
    width = gains.shape[1]
    heads = cols // (3 * width)
    per = 2 if heads % 2 == 0 else 1
    rows = 4 * x0.shape[0]
    whole = lambda a: pl.BlockSpec(a.shape, lambda j: (0,) * a.ndim)
    small = (x0, x1, embed_weight, embed_bias[None], shift[None], scale[None], gains)
    out = jax.ShapeDtypeStruct((rows, heads * width), BF16)
    ospec = pl.BlockSpec((rows, per * width), lambda j: (0, j))
    return pl.pallas_call(
        functools.partial(project_kernel, chunk=min(128, x0.shape[0]), width=width),
        grid=(heads // per,),
        in_specs=[whole(a) for a in small]
        + [pl.BlockSpec((d, per * 3 * width), lambda j: (0, j))],
        out_specs=[ospec] * 3,
        out_shape=[out] * 3,
        scratch_shapes=[pltpu.VMEM((rows, d), BF16)],
        compiler_params=pltpu.CompilerParams(vmem_limit_bytes=44 * 1024 * 1024),
        cost_estimate=pl.CostEstimate(
            flops=2 * rows * d * cols, bytes_accessed=2 * d * cols + 6 * rows * heads * width,
            transcendentals=0),
        name="project",
    )(*small, weight)


def image_kernel(q_ref, k_ref, v_ref, acc_ref, sum_ref, *, chunk, unit):
    width = k_ref.shape[1]
    vals = jnp.concatenate([v_ref[...], jnp.ones_like(v_ref)], axis=1)
    for at in range(0, q_ref.shape[0], chunk):
        r = slice(at, at + chunk)
        s = lax.dot_general(q_ref[r, :], k_ref[...], NT, preferred_element_type=F32)
        p = jnp.exp2(s * unit).astype(BF16)
        o = jnp.dot(p, vals, preferred_element_type=F32)
        acc_ref[r, :] = o[:, :width]
        sum_ref[r, :] = o[:, width:]


def image_attention(q, k, v, half, width):
    tokens, cols = q.shape
    rows = tokens // 2
    heads = cols // width
    unit = LOG2E / width ** 0.5
    out = jax.ShapeDtypeStruct((rows, cols), F32)
    return pl.pallas_call(
        functools.partial(image_kernel, chunk=256, unit=unit),
        grid=(heads,),
        in_specs=[pl.BlockSpec((rows, width), lambda h: (half, h))]
        + [pl.BlockSpec((tokens, width), lambda h: (0, h))] * 2,
        out_specs=[pl.BlockSpec((rows, width), lambda h: (0, h))] * 2,
        out_shape=[out] * 2,
        compiler_params=pltpu.CompilerParams(vmem_limit_bytes=32 * 1024 * 1024),
        cost_estimate=pl.CostEstimate(
            flops=8 * rows * tokens * cols, bytes_accessed=6 * tokens * cols + 8 * rows * cols,
            transcendentals=rows * tokens * heads),
        name=f"image_{half}",
    )(q, k, v)


def text_kernel(q_ref, ka_ref, kb_ref, va_ref, vb_ref, acc_ref, sum_ref, out_ref, *, unit):
    width = ka_ref.shape[1]
    keys = jnp.concatenate([ka_ref[...], kb_ref[...]], axis=0)
    vals = jnp.concatenate([va_ref[...], vb_ref[...]], axis=0)
    vals = jnp.concatenate([vals, jnp.ones_like(vals)], axis=1)
    s = lax.dot_general(q_ref[...], keys, NT, preferred_element_type=F32) * unit
    top = jnp.maximum(jnp.max(s, axis=-1, keepdims=True), 0.0)
    p = jnp.exp2(s - top).astype(BF16)
    o = jnp.dot(p, vals, preferred_element_type=F32)
    fade = jnp.exp2(-top)
    total = sum_ref[...] * fade + o[:, width:]
    out_ref[...] = ((acc_ref[...] * fade + o[:, :width]) / total).astype(BF16)


def text_attention(q, ka, kb, va, vb, acc, total, half, width):
    tokens, cols = q.shape
    rows = tokens // 2
    heads = cols // width
    unit = LOG2E / width ** 0.5
    part = pl.BlockSpec((ka.shape[0], width), lambda h: (0, h))
    full = pl.BlockSpec((rows, width), lambda h: (0, h))
    return pl.pallas_call(
        functools.partial(text_kernel, unit=unit),
        grid=(heads,),
        in_specs=[pl.BlockSpec((rows, width), lambda h: (half, h))] + [part] * 4 + [full] * 2,
        out_specs=full,
        out_shape=jax.ShapeDtypeStruct((rows, cols), BF16),
        compiler_params=pltpu.CompilerParams(vmem_limit_bytes=32 * 1024 * 1024),
        cost_estimate=pl.CostEstimate(
            flops=16 * rows * ka.shape[0] * cols, bytes_accessed=14 * rows * cols,
            transcendentals=2 * rows * ka.shape[0] * heads),
        name=f"text_{half}",
    )(q, ka, kb, va, vb, acc, total)


def pack(lat):
    rows = lat.shape[0] // 2
    return jnp.concatenate([lat[:rows], lat[rows:]], axis=1)


def pick(which, choices):
    res = choices[0]
    for i, item in enumerate(choices[1:], 1):
        res = jnp.where(which == i, item, res)
    return res


def route_latents(lat, chosen, me):
    z, y = me // 2, me % 2
    held = [lat]
    for k in (1, 2, 3):
        held.append(lax.ppermute(
            lat, "particle", [(2 * a + b, 2 * ((a + k) % 4) + b) for a in range(4) for b in range(2)]))
    need = chosen[me]
    other = chosen[me ^ 1]
    mine = pick((z - need // 2) % 4, held)
    theirs = pick((z - other // 2) % 4, held)
    swap = [(p, p ^ 1) for p in range(8)]
    flip = [(0, 1), (1, 0)]
    diag = [(2 * p + s, 2 * (p ^ 1) + (1 - s)) for p in range(8) for s in range(2)]
    from_y = lax.ppermute(theirs, "particle", swap)
    from_seq = lax.ppermute(mine, "seq", flip)
    from_diag = lax.ppermute(theirs, ("particle", "seq"), diag)
    here = need % 2 == y
    return jnp.where(here, from_seq, from_diag), jnp.where(here, mine, from_y)


def route_text(kv, chosen, me, after):
    z, y = me // 2, me % 2
    swap = [(p, p ^ 1) for p in range(8)]
    middle = [(2, 4), (3, 5), (4, 2), (5, 3)]
    inward = [(0, 2), (1, 3), (6, 4), (7, 5)]
    beyond = [(0, 4), (1, 5), (6, 2), (7, 3)]
    outward = [(2, 0), (3, 1), (4, 6), (5, 7)]
    rows = kv.shape[1] // 2
    got = []
    plane = jnp.where(z < 2, 0, 3)
    planes = []
    for c in range(2):
        halves = kv[c].reshape(2, rows, kv.shape[2])
        own = jnp.where(y == 0, halves[0], halves[1])
        give = jnp.where(y == 0, halves[1], halves[0])
        recv = lax.ppermute(give, "particle", swap)
        planes.append(jnp.stack([jnp.where(y == 0, own, recv), jnp.where(y == 0, recv, own)]))
    planes, _ = lax.optimization_barrier((planes, after))
    for c in range(2):
        own = planes[c]
        held = [own, lax.ppermute(own, "particle", middle),
                lax.ppermute(own, "particle", inward), lax.ppermute(own, "particle", beyond)]

        def find(need):
            at = need // 2
            which = jnp.where(at == z, 0, jnp.where(at == 3 - z, 1, jnp.where(at == plane, 2, 3)))
            row = need % 2
            return pick(which, [jnp.where(row == 0, h[0], h[1]) for h in held])

        out = jnp.stack([find(jnp.where(z < 2, chosen[i], chosen[6 + i])) for i in range(2)])
        sent = lax.ppermute(out, "particle", outward)
        inner = (z == 1) | (z == 2)

        def final(slot):
            need = chosen[slot]
            edge = jnp.where(need // 2 == z, jnp.where(need % 2 == 0, own[0], own[1]),
                             jnp.where(slot % 2 == 0, sent[0], sent[1]))
            return jnp.where(inner, find(need), edge)

        mine = final(me)
        got.append((mine, lax.ppermute(final(me ^ 1), "particle", swap)))
    return got


def body(latents, text_kv, ancestors, order, embed_weight, embed_bias, shift, scale,
         qkv_weight, norm_gains, *, particles):
    width = norm_gains.shape[1]
    me = lax.axis_index("particle")
    seq = lax.axis_index("seq")
    chosen = ancestors[order]
    lat = pack(latents[0].astype(BF16))
    kv = text_kv[0]
    if particles == 8:
        x_other, x_mine = route_latents(lat, chosen, me)
        (ka, kb), (va, vb) = route_text(kv, chosen, me, x_mine)
    else:
        need = chosen[me]
        x_mine = lax.all_gather(lat, "particle", axis=0)[need]
        x_other = lax.ppermute(x_mine, "seq", [(0, 1), (1, 0)])
        text = lax.all_gather(kv, "particle", axis=0)[need]
        rows = text.shape[1] // 2
        ka, kb, va, vb = text[0, :rows], text[0, rows:], text[1, :rows], text[1, rows:]
    q, k, v = project(x_other, x_mine, embed_weight, embed_bias, shift, scale, norm_gains, qkv_weight)
    acc0, sum0 = image_attention(q, k, v, 0, width)
    acc1, sum1 = image_attention(q, k, v, 1, width)
    away = text_attention(q, ka, kb, va, vb, acc0, sum0, 0, width)
    theirs = lax.ppermute(away, "seq", [(0, 1), (1, 0)])
    mine = text_attention(q, ka, kb, va, vb, acc1, sum1, 1, width)
    left = jnp.where(seq == 0, mine, theirs)
    right = jnp.where(seq == 0, theirs, mine)
    return jnp.concatenate([left, right], axis=1)[None]


def solution(mesh):
    in_specs = (
        P(("groups", "particle"), "seq", None),
        P(("groups", "particle"), None, None, "seq"),
        P("groups"),
        P("groups"),
        P(),
        P(),
        P("groups"),
        P("groups"),
        P(None, "seq"),
        P(),
    )
    out_specs = P(("groups", "particle"), "seq", None)
    run = functools.partial(body, particles=mesh.shape["particle"])
    return jax.shard_map(run, mesh=mesh, in_specs=in_specs, out_specs=out_specs, check_vma=False)
```

```python
import functools
import jax
import jax.numpy as jnp
from jax import lax
from jax.experimental import pallas as pl
from jax.experimental.pallas import tpu as pltpu
from jax.sharding import PartitionSpec as P

LOG2E = 1.4426950408889634
BF16 = jnp.bfloat16
F32 = jnp.float32
NT = (((1,), (1,)), ((), ()))


def rms_norm(values, gain):
    return values * lax.rsqrt(jnp.mean(values * values, axis=-1, keepdims=True) + 1e-06) * gain


def project_kernel(x0_ref, x1_ref, ew_ref, eb_ref, sh_ref, sc_ref, gain_ref, w_ref,
                   q_ref, k_ref, v_ref, normed, *, chunk, width):
    half = x0_ref.shape[0] * 2
    lanes = x0_ref.shape[1] // 2

    @pl.when(pl.program_id(0) == 0)
    def _():
        for part, x_ref in enumerate((x0_ref, x1_ref)):
            for side in range(2):
                for at in range(0, half // 2, chunk):
                    x = x_ref[at:at + chunk, side * lanes:(side + 1) * lanes]
                    emb = jnp.dot(x, ew_ref[...], preferred_element_type=F32) + eb_ref[...]
                    center = emb - jnp.mean(emb, axis=-1, keepdims=True)
                    spread = jnp.mean(center * center, axis=-1, keepdims=True)
                    res = center * lax.rsqrt(spread + 1e-06) * (1.0 + sc_ref[...]) + sh_ref[...]
                    row = part * half + side * (half // 2) + at
                    normed[row:row + chunk, :] = res.astype(BF16)

    rows = normed.shape[0]
    heads = w_ref.shape[1] // (3 * width)
    step = 256

    @pl.loop(0, rows // step)
    def _(i):
        r = pl.ds(pl.multiple_of(i * step, step), step)
        mixed = jnp.dot(normed[r, :], w_ref[...], preferred_element_type=F32)
        for h in range(heads):
            c = slice(h * width, (h + 1) * width)
            base = h * 3 * width
            q_ref[r, c] = rms_norm(mixed[:, base:base + width], gain_ref[0:1, :]).astype(BF16)
            k_ref[r, c] = rms_norm(
                mixed[:, base + width:base + 2 * width], gain_ref[1:2, :]
            ).astype(BF16)
            v_ref[r, c] = mixed[:, base + 2 * width:base + 3 * width].astype(BF16)


def project(x0, x1, embed_weight, embed_bias, shift, scale, gains, weight):
    d, cols = weight.shape
    width = gains.shape[1]
    heads = cols // (3 * width)
    per = 2 if heads % 2 == 0 else 1
    rows = 4 * x0.shape[0]
    whole = lambda a: pl.BlockSpec(a.shape, lambda j: (0,) * a.ndim)
    small = (x0, x1, embed_weight, embed_bias[None], shift[None], scale[None], gains)
    out = jax.ShapeDtypeStruct((rows, heads * width), BF16)
    ospec = pl.BlockSpec((rows, per * width), lambda j: (0, j))
    return pl.pallas_call(
        functools.partial(project_kernel, chunk=min(128, x0.shape[0]), width=width),
        grid=(heads // per,),
        in_specs=[whole(a) for a in small]
        + [pl.BlockSpec((d, per * 3 * width), lambda j: (0, j))],
        out_specs=[ospec] * 3,
        out_shape=[out] * 3,
        scratch_shapes=[pltpu.VMEM((rows, d), BF16)],
        compiler_params=pltpu.CompilerParams(vmem_limit_bytes=44 * 1024 * 1024),
        cost_estimate=pl.CostEstimate(
            flops=2 * rows * d * cols, bytes_accessed=2 * d * cols + 6 * rows * heads * width,
            transcendentals=0),
        name="project",
    )(*small, weight)


def image_alone_kernel(q_ref, k_ref, v_ref, acc_ref, sum_ref, *, chunk, unit):
    width = k_ref.shape[1]
    vals = jnp.concatenate([v_ref[...], jnp.ones_like(v_ref)], axis=1)
    for at in range(0, q_ref.shape[0], chunk):
        r = slice(at, at + chunk)
        s = lax.dot_general(q_ref[r, :], k_ref[...], NT, preferred_element_type=F32)
        p = jnp.exp2(s * unit).astype(BF16)
        o = jnp.dot(p, vals, preferred_element_type=F32)
        acc_ref[r, :] = o[:, :width]
        sum_ref[r, :] = o[:, width:]


def image_alone(q, k, v, width):
    tokens, cols = q.shape
    head = pl.BlockSpec((tokens, width), lambda h: (0, h))
    out = jax.ShapeDtypeStruct((tokens, cols), F32)
    return pl.pallas_call(
        functools.partial(image_alone_kernel, chunk=256, unit=LOG2E / width ** 0.5),
        grid=(cols // width,),
        in_specs=[head] * 3,
        out_specs=[head] * 2,
        out_shape=[out] * 2,
        compiler_params=pltpu.CompilerParams(vmem_limit_bytes=32 * 1024 * 1024),
        name="image_alone",
    )(q, k, v)


def text_kernel(q_ref, ka_ref, kb_ref, va_ref, vb_ref, acc_ref, sum_ref, out_ref, *, unit):
    width = ka_ref.shape[1]
    keys = jnp.concatenate([ka_ref[...], kb_ref[...]], axis=0)
    vals = jnp.concatenate([va_ref[...], vb_ref[...]], axis=0)
    vals = jnp.concatenate([vals, jnp.ones_like(vals)], axis=1)
    s = lax.dot_general(q_ref[...], keys, NT, preferred_element_type=F32) * unit
    top = jnp.maximum(jnp.max(s, axis=-1, keepdims=True), 0.0)
    p = jnp.exp2(s - top).astype(BF16)
    o = jnp.dot(p, vals, preferred_element_type=F32)
    fade = jnp.exp2(-top)
    total = sum_ref[...] * fade + o[:, width:]
    out_ref[...] = ((acc_ref[...] * fade + o[:, :width]) / total).astype(BF16)


def text_attention(q, ka, kb, va, vb, acc, total, half, width):
    tokens, cols = q.shape
    rows = tokens // 2
    heads = cols // width
    unit = LOG2E / width ** 0.5
    part = pl.BlockSpec((ka.shape[0], width), lambda h: (0, h))
    full = pl.BlockSpec((rows, width), lambda h: (0, h))
    return pl.pallas_call(
        functools.partial(text_kernel, unit=unit),
        grid=(heads,),
        in_specs=[pl.BlockSpec((rows, width), lambda h: (half, h))] + [part] * 4
        + [pl.BlockSpec((rows, width), lambda h: (half, h))] * 2,
        out_specs=full,
        out_shape=jax.ShapeDtypeStruct((rows, cols), BF16),
        compiler_params=pltpu.CompilerParams(vmem_limit_bytes=32 * 1024 * 1024),
        cost_estimate=pl.CostEstimate(
            flops=16 * rows * ka.shape[0] * cols, bytes_accessed=14 * rows * cols,
            transcendentals=2 * rows * ka.shape[0] * heads),
        name=f"text_{half}",
    )(q, ka, kb, va, vb, acc, total)


def pack(lat):
    rows = lat.shape[0] // 2
    return jnp.concatenate([lat[:rows], lat[rows:]], axis=1)


MESH = pl.DeviceIdType.MESH


def greet(peers):
    barrier = pltpu.get_barrier_semaphore()
    for peer in peers:
        pl.semaphore_signal(barrier, inc=1, device_id=peer, device_id_type=MESH)
    pl.semaphore_wait(barrier, len(peers))


def gather_kernel(anc_ref, ord_ref, lat_ref, kv_ref, other_ref, mine_ref, plane_ref,
                  held, give, keep, send, recv, local):
    g, me, s = lax.axis_index("groups"), lax.axis_index("particle"), lax.axis_index("seq")
    z, y = me // 2, me % 2
    across = (g, 2 * z + 1 - y, s)
    core = (g, me, 1 - s)
    diag = (g, 2 * z + 1 - y, 1 - s)
    planes = [(g, 2 * ((z + k) % 4) + y, s) for k in (1, 2, 3)]
    greet(planes + [across, core, diag])

    def push(src, dst, i, peer):
        return pltpu.make_async_remote_copy(
            src_ref=src, dst_ref=dst, send_sem=send.at[i], recv_sem=recv.at[i],
            device_id=peer, device_id_type=MESH)

    first = [push(lat_ref, held.at[k], k - 1, planes[k - 1]) for k in (1, 2, 3)]
    for copy in first:
        copy.start()
    rows = kv_ref.shape[1] // 2
    text = push(kv_ref.at[:, pl.ds(pl.multiple_of((1 - y) * rows, rows), rows)],
                plane_ref.at[:, y], 3, across)
    text.start()
    own = pltpu.make_async_copy(
        kv_ref.at[:, pl.ds(pl.multiple_of(y * rows, rows), rows)], plane_ref.at[:, y], local)
    own.start()
    held[0] = lat_ref[...]
    need = anc_ref[ord_ref[me]]
    wish = anc_ref[ord_ref[2 * z + 1 - y]]
    for copy in first:
        copy.wait()
    keep[0] = held[(z + 4 - need // 2) % 4]
    give[...] = held[(z + 4 - wish // 2) % 4]
    second = [push(give, keep.at[1], 4, across), push(keep.at[0], keep.at[2], 5, core),
              push(give, keep.at[3], 6, diag)]
    for copy in second:
        copy.start()
    for copy in second:
        copy.wait()
    turn = (need % 2 + y) % 2
    mine_ref[...] = keep[turn]
    other_ref[...] = keep[2 + turn]
    text.wait()
    own.wait()


def gather(ancestors, order, lat, kv):
    block = jax.ShapeDtypeStruct(lat.shape, lat.dtype)
    two, rows, cols = kv.shape
    vmem = pl.BlockSpec(memory_space=pltpu.VMEM)
    smem = pl.BlockSpec(memory_space=pltpu.SMEM)
    anyp = pl.BlockSpec(memory_space=pl.ANY)
    return pl.pallas_call(
        gather_kernel,
        in_specs=[smem, smem, vmem, anyp],
        out_specs=[vmem, vmem, anyp],
        out_shape=[block, block, jax.ShapeDtypeStruct((two, 2, rows // 2, cols), kv.dtype)],
        scratch_shapes=[pltpu.VMEM((4,) + lat.shape, lat.dtype), pltpu.VMEM(lat.shape, lat.dtype),
                        pltpu.VMEM((4,) + lat.shape, lat.dtype),
                        pltpu.SemaphoreType.DMA((7,)), pltpu.SemaphoreType.DMA((7,)),
                        pltpu.SemaphoreType.DMA],
        compiler_params=pltpu.CompilerParams(
            collective_id=0, has_side_effects=True, vmem_limit_bytes=16 * 1024 * 1024),
        cost_estimate=pl.CostEstimate(flops=0, bytes_accessed=20000000, transcendentals=0),
        name="gather",
    )(ancestors, order, lat, kv)


def inward_planes(planes):
    middle = [(2, 4), (3, 5), (4, 2), (5, 3)]
    inward = [(0, 2), (1, 3), (6, 4), (7, 5)]
    beyond = [(0, 4), (1, 5), (6, 2), (7, 3)]
    return [lax.ppermute(planes, "particle", pairs) for pairs in (middle, inward, beyond)]


def image_kernel(anc_ref, ord_ref, own_ref, mid_ref, in_ref, far_ref, q_ref, k_ref, v_ref,
                 acc_ref, sum_ref, mine_ref, theirs_ref,
                 outward, landed, give, came, send, recv, *, chunk, unit):
    g, me, s = lax.axis_index("groups"), lax.axis_index("particle"), lax.axis_index("seq")
    step = pl.program_id(0)
    z, y = me // 2, me % 2
    inner = jnp.logical_or(z == 1, z == 2)
    edge = jnp.where(z < 2, 0, 3)
    beside = jnp.where(z == 0, 1, jnp.where(z == 1, 0, jnp.where(z == 2, 3, 2)))
    across = (g, 2 * z + 1 - y, s)
    along = (g, 2 * beside + y, s)

    def out_copy(c):
        return pltpu.make_async_remote_copy(
            src_ref=outward.at[c], dst_ref=landed.at[c], send_sem=send.at[c], recv_sem=recv.at[c],
            device_id=along, device_id_type=MESH)

    def swap_copy(c):
        return pltpu.make_async_remote_copy(
            src_ref=give.at[c], dst_ref=came.at[c], send_sem=send.at[2 + c],
            recv_sem=recv.at[2 + c], device_id=across, device_id_type=MESH)

    def find(c, need):
        at, row = need // 2, need % 2
        which = jnp.where(at == z, 0, jnp.where(at == 3 - z, 1, jnp.where(at == edge, 2, 3)))
        res = own_ref[c, row]
        for i, ref in enumerate((mid_ref, in_ref, far_ref), 1):
            res = jnp.where(which == i, ref[c, row], res)
        return res

    need_mine = anc_ref[ord_ref[me]]
    need_give = anc_ref[ord_ref[2 * z + 1 - y]]

    def finish(c):
        for ref, need, slot in ((mine_ref, need_mine, y), (give, need_give, 1 - y)):
            ref[c] = jnp.where(need // 2 == z, own_ref[c, need % 2], landed[c, slot])
        swap_copy(c).start()

    @pl.when(step == 0)
    def _():
        greet([across, along])

        @pl.when(inner)
        def _():
            for c in range(2):
                for i in range(2):
                    outward[c, i] = find(c, anc_ref[ord_ref[2 * edge + i]])
                out_copy(c).start()
            for c in range(2):
                mine_ref[c] = find(c, need_mine)
                give[c] = find(c, need_give)
                swap_copy(c).start()

    width = k_ref.shape[1]
    vals = jnp.concatenate([v_ref[...], jnp.ones_like(v_ref)], axis=1)
    for at in range(0, q_ref.shape[0], chunk):
        r = slice(at, at + chunk)
        sc = lax.dot_general(q_ref[r, :], k_ref[...], NT, preferred_element_type=F32)
        p = jnp.exp2(sc * unit).astype(BF16)
        o = jnp.dot(p, vals, preferred_element_type=F32)
        acc_ref[r, :] = o[:, :width]
        sum_ref[r, :] = o[:, width:]

    last = pl.num_programs(0) - 1

    @pl.when(jnp.logical_and(step == last - 1, jnp.logical_not(inner)))
    def _():
        out_copy(0).wait_recv()
        finish(0)

    @pl.when(step == last)
    def _():
        @pl.when(jnp.logical_not(inner))
        def _():
            out_copy(1).wait_recv()
            finish(1)

        @pl.when(inner)
        def _():
            for c in range(2):
                out_copy(c).wait_send()

        for c in range(2):
            swap_copy(c).wait()
            theirs_ref[c] = came[c]


def image_attention(ancestors, order, own, others, q, k, v, width):
    tokens, cols = q.shape
    heads = cols // width
    unit = LOG2E / width ** 0.5
    out = jax.ShapeDtypeStruct((tokens, cols), F32)
    two, _, rows, _ = own.shape
    text = jax.ShapeDtypeStruct((two, rows, cols), BF16)
    vmem = pl.BlockSpec(memory_space=pltpu.VMEM)
    smem = pl.BlockSpec(memory_space=pltpu.SMEM)
    head = pl.BlockSpec((tokens, width), lambda h: (0, h))
    return pl.pallas_call(
        functools.partial(image_kernel, chunk=256, unit=unit),
        grid=(heads,),
        in_specs=[smem, smem] + [vmem] * 4 + [head] * 3,
        out_specs=[head, head, vmem, vmem],
        out_shape=[out, out, text, text],
        scratch_shapes=[pltpu.VMEM(own.shape, BF16), pltpu.VMEM(own.shape, BF16),
                        pltpu.VMEM(text.shape, BF16), pltpu.VMEM(text.shape, BF16),
                        pltpu.SemaphoreType.DMA((4,)), pltpu.SemaphoreType.DMA((4,))],
        compiler_params=pltpu.CompilerParams(
            collective_id=1, has_side_effects=True, vmem_limit_bytes=40 * 1024 * 1024),
        cost_estimate=pl.CostEstimate(
            flops=8 * tokens * tokens * cols, bytes_accessed=14 * tokens * cols,
            transcendentals=tokens * tokens * heads),
        name="image",
    )(ancestors, order, own, *others, q, k, v)


def body(latents, text_kv, ancestors, order, embed_weight, embed_bias, shift, scale,
         qkv_weight, norm_gains, *, particles):
    width = norm_gains.shape[1]
    seq = lax.axis_index("seq")
    lat = pack(latents[0].astype(BF16))
    kv = text_kv[0]
    small = (embed_weight, embed_bias, shift, scale, norm_gains, qkv_weight)
    if particles == 8:
        x_other, x_mine, planes = gather(ancestors, order, lat, kv)
        others = inward_planes(planes)
        q, k, v = project(x_other, x_mine, *small)
        acc, total, own, swapped = image_attention(ancestors, order, planes, others, q, k, v, width)
        (ka, va), (kb, vb) = own, swapped
    else:
        need = ancestors[order][lax.axis_index("particle")]
        x_mine = lax.all_gather(lat, "particle", axis=0)[need]
        x_other = lax.ppermute(x_mine, "seq", [(0, 1), (1, 0)])
        text = lax.all_gather(kv, "particle", axis=0)[need]
        rows = text.shape[1] // 2
        ka, kb, va, vb = text[0, :rows], text[0, rows:], text[1, :rows], text[1, rows:]
        q, k, v = project(x_other, x_mine, *small)
        acc, total = image_alone(q, k, v, width)
    away = text_attention(q, ka, kb, va, vb, acc, total, 0, width)
    theirs = lax.ppermute(away, "seq", [(0, 1), (1, 0)])
    mine = text_attention(q, ka, kb, va, vb, acc, total, 1, width)
    left = jnp.where(seq == 0, mine, theirs)
    right = jnp.where(seq == 0, theirs, mine)
    return jnp.concatenate([left, right], axis=1)[None]


def solution(mesh):
    in_specs = (
        P(("groups", "particle"), "seq", None),
        P(("groups", "particle"), None, None, "seq"),
        P("groups"),
        P("groups"),
        P(),
        P(),
        P("groups"),
        P("groups"),
        P(None, "seq"),
        P(),
    )
    out_specs = P(("groups", "particle"), "seq", None)
    run = functools.partial(body, particles=mesh.shape["particle"])
    return jax.shard_map(run, mesh=mesh, in_specs=in_specs, out_specs=out_specs, check_vma=False)
```

```python
import functools
import jax
import jax.numpy as jnp
from jax import lax
from jax.experimental import pallas as pl
from jax.experimental.pallas import tpu as pltpu
from jax.sharding import PartitionSpec as P

LOG2E = 1.4426950408889634
BF16 = jnp.bfloat16
F32 = jnp.float32
NT = (((1,), (1,)), ((), ()))


def rms_norm(values, gain):
    return values * lax.rsqrt(jnp.mean(values * values, axis=-1, keepdims=True) + 1e-06) * gain


def project_kernel(x0_ref, x1_ref, ew_ref, eb_ref, sh_ref, sc_ref, gain_ref, w_ref,
                   q_ref, k_ref, v_ref, normed, *, chunk, width):
    half = x0_ref.shape[0] * 2
    lanes = x0_ref.shape[1] // 2

    @pl.when(pl.program_id(0) == 0)
    def _():
        for part, x_ref in enumerate((x0_ref, x1_ref)):
            for side in range(2):
                for at in range(0, half // 2, chunk):
                    x = x_ref[at:at + chunk, side * lanes:(side + 1) * lanes]
                    emb = jnp.dot(x, ew_ref[...], preferred_element_type=F32) + eb_ref[...]
                    center = emb - jnp.mean(emb, axis=-1, keepdims=True)
                    spread = jnp.mean(center * center, axis=-1, keepdims=True)
                    res = center * lax.rsqrt(spread + 1e-06) * (1.0 + sc_ref[...]) + sh_ref[...]
                    row = part * half + side * (half // 2) + at
                    normed[row:row + chunk, :] = res.astype(BF16)

    rows = normed.shape[0]
    heads = w_ref.shape[1] // (3 * width)
    step = 256

    @pl.loop(0, rows // step)
    def _(i):
        r = pl.ds(pl.multiple_of(i * step, step), step)
        mixed = jnp.dot(normed[r, :], w_ref[...], preferred_element_type=F32)
        for h in range(heads):
            c = slice(h * width, (h + 1) * width)
            base = h * 3 * width
            q_ref[r, c] = rms_norm(mixed[:, base:base + width], gain_ref[0:1, :]).astype(BF16)
            k_ref[r, c] = rms_norm(
                mixed[:, base + width:base + 2 * width], gain_ref[1:2, :]
            ).astype(BF16)
            v_ref[r, c] = mixed[:, base + 2 * width:base + 3 * width].astype(BF16)


def project(x0, x1, embed_weight, embed_bias, shift, scale, gains, weight, route=None):
    d, cols = weight.shape
    width = gains.shape[1]
    heads = cols // (3 * width)
    per = 2 if heads % 2 == 0 else 1
    rows = 4 * x0.shape[0]
    whole = lambda a: pl.BlockSpec(a.shape, lambda j: (0,) * a.ndim)
    small = (x0, x1, embed_weight, embed_bias[None], shift[None], scale[None], gains)
    out = jax.ShapeDtypeStruct((rows, heads * width), BF16)
    ospec = pl.BlockSpec((rows, per * width), lambda j: (0, j))
    cost = pl.CostEstimate(
        flops=2 * rows * d * cols, bytes_accessed=2 * d * cols + 6 * rows * heads * width,
        transcendentals=0)
    chunk = min(128, x0.shape[0])
    in_specs = [whole(a) for a in small] + [pl.BlockSpec((d, per * 3 * width), lambda j: (0, j))]
    scratch = [pltpu.VMEM((rows, d), BF16)]
    if route is None:
        return pl.pallas_call(
            functools.partial(project_kernel, chunk=chunk, width=width),
            grid=(heads // per,),
            in_specs=in_specs,
            out_specs=[ospec] * 3,
            out_shape=[out] * 3,
            scratch_shapes=scratch,
            compiler_params=pltpu.CompilerParams(vmem_limit_bytes=44 * 1024 * 1024),
            cost_estimate=cost,
            name="project",
        )(*small, weight)
    own = route[2]
    vmem = pl.BlockSpec(memory_space=pltpu.VMEM)
    smem = pl.BlockSpec(memory_space=pltpu.SMEM)
    three = (3,) + own.shape
    half = own.shape[1:]
    return pl.pallas_call(
        functools.partial(routed_kernel, chunk=chunk, width=width),
        grid=(heads // per,),
        in_specs=[smem, smem, vmem] + in_specs,
        out_specs=[ospec] * 3 + [vmem] * 2,
        out_shape=[out] * 3 + [jax.ShapeDtypeStruct(three, BF16), jax.ShapeDtypeStruct(half, BF16)],
        scratch_shapes=scratch + [
            pltpu.VMEM((3,) + half, BF16), pltpu.VMEM((3,) + half, BF16),
            pltpu.VMEM(half, BF16), pltpu.VMEM(half, BF16),
            pltpu.SemaphoreType.DMA((7,)), pltpu.SemaphoreType.DMA((7,))],
        compiler_params=pltpu.CompilerParams(
            collective_id=2, has_side_effects=True, vmem_limit_bytes=58 * 1024 * 1024),
        cost_estimate=cost,
        name="project_routed",
    )(*route, *small, weight)


def image_alone_kernel(q_ref, k_ref, v_ref, acc_ref, sum_ref, *, chunk, unit):
    width = k_ref.shape[1]
    vals = jnp.concatenate([v_ref[...], jnp.ones_like(v_ref)], axis=1)
    for at in range(0, q_ref.shape[0], chunk):
        r = slice(at, at + chunk)
        s = lax.dot_general(q_ref[r, :], k_ref[...], NT, preferred_element_type=F32)
        p = jnp.exp2(s * unit).astype(BF16)
        o = jnp.dot(p, vals, preferred_element_type=F32)
        acc_ref[r, :] = o[:, :width]
        sum_ref[r, :] = o[:, width:]


def image_alone(q, k, v, width):
    tokens, cols = q.shape
    head = pl.BlockSpec((tokens, width), lambda h: (0, h))
    out = jax.ShapeDtypeStruct((tokens, cols), F32)
    return pl.pallas_call(
        functools.partial(image_alone_kernel, chunk=256, unit=LOG2E / width ** 0.5),
        grid=(cols // width,),
        in_specs=[head] * 3,
        out_specs=[head] * 2,
        out_shape=[out] * 2,
        compiler_params=pltpu.CompilerParams(vmem_limit_bytes=58 * 1024 * 1024),
        name="image_alone",
    )(q, k, v)


def text_kernel(q_ref, ka_ref, kb_ref, va_ref, vb_ref, acc_ref, sum_ref, out_ref, *, unit):
    width = ka_ref.shape[1]
    keys = jnp.concatenate([ka_ref[...], kb_ref[...]], axis=0)
    vals = jnp.concatenate([va_ref[...], vb_ref[...]], axis=0)
    vals = jnp.concatenate([vals, jnp.ones_like(vals)], axis=1)
    s = lax.dot_general(q_ref[...], keys, NT, preferred_element_type=F32) * unit
    top = jnp.maximum(jnp.max(s, axis=-1, keepdims=True), 0.0)
    p = jnp.exp2(s - top).astype(BF16)
    o = jnp.dot(p, vals, preferred_element_type=F32)
    fade = jnp.exp2(-top)
    total = sum_ref[...] * fade + o[:, width:]
    out_ref[...] = ((acc_ref[...] * fade + o[:, :width]) / total).astype(BF16)


def text_attention(q, ka, kb, va, vb, acc, total, half, width):
    tokens, cols = q.shape
    rows = tokens // 2
    heads = cols // width
    unit = LOG2E / width ** 0.5
    part = pl.BlockSpec((ka.shape[0], width), lambda h: (0, h))
    full = pl.BlockSpec((rows, width), lambda h: (0, h))
    return pl.pallas_call(
        functools.partial(text_kernel, unit=unit),
        grid=(heads,),
        in_specs=[pl.BlockSpec((rows, width), lambda h: (half, h))] + [part] * 4
        + [pl.BlockSpec((rows, width), lambda h: (half, h))] * 2,
        out_specs=full,
        out_shape=jax.ShapeDtypeStruct((rows, cols), BF16),
        compiler_params=pltpu.CompilerParams(vmem_limit_bytes=58 * 1024 * 1024),
        cost_estimate=pl.CostEstimate(
            flops=16 * rows * ka.shape[0] * cols, bytes_accessed=14 * rows * cols,
            transcendentals=2 * rows * ka.shape[0] * heads),
        name=f"text_{half}",
    )(q, ka, kb, va, vb, acc, total)


def pack(lat):
    rows = lat.shape[0] // 2
    return jnp.concatenate([lat[:rows], lat[rows:]], axis=1)


MESH = pl.DeviceIdType.MESH


def greet(peers):
    barrier = pltpu.get_barrier_semaphore()
    for peer in peers:
        pl.semaphore_signal(barrier, inc=1, device_id=peer, device_id_type=MESH)
    pl.semaphore_wait(barrier, len(peers))


def gather_kernel(anc_ref, ord_ref, lat_ref, kv_ref, other_ref, mine_ref, plane_ref,
                  held, give, keep, send, recv, local):
    g, me, s = lax.axis_index("groups"), lax.axis_index("particle"), lax.axis_index("seq")
    z, y = me // 2, me % 2
    across = (g, 2 * z + 1 - y, s)
    core = (g, me, 1 - s)
    diag = (g, 2 * z + 1 - y, 1 - s)
    planes = [(g, 2 * ((z + k) % 4) + y, s) for k in (1, 2, 3)]
    greet(planes + [across, core, diag])

    def push(src, dst, i, peer):
        return pltpu.make_async_remote_copy(
            src_ref=src, dst_ref=dst, send_sem=send.at[i], recv_sem=recv.at[i],
            device_id=peer, device_id_type=MESH)

    first = [push(lat_ref, held.at[k], k - 1, planes[k - 1]) for k in (1, 2, 3)]
    for copy in first:
        copy.start()
    rows = kv_ref.shape[1] // 2
    text = push(kv_ref.at[:, pl.ds(pl.multiple_of((1 - y) * rows, rows), rows)],
                plane_ref.at[:, y], 3, across)
    text.start()
    own = pltpu.make_async_copy(
        kv_ref.at[:, pl.ds(pl.multiple_of(y * rows, rows), rows)], plane_ref.at[:, y], local)
    own.start()
    held[0] = lat_ref[...]
    need = anc_ref[ord_ref[me]]
    wish = anc_ref[ord_ref[2 * z + 1 - y]]
    for copy in first:
        copy.wait()
    keep[0] = held[(z + 4 - need // 2) % 4]
    give[...] = held[(z + 4 - wish // 2) % 4]
    second = [push(give, keep.at[1], 4, across), push(keep.at[0], keep.at[2], 5, core),
              push(give, keep.at[3], 6, diag)]
    for copy in second:
        copy.start()
    for copy in second:
        copy.wait()
    turn = (need % 2 + y) % 2
    mine_ref[...] = keep[turn]
    other_ref[...] = keep[2 + turn]
    text.wait()
    own.wait()


def gather(ancestors, order, lat, kv):
    block = jax.ShapeDtypeStruct(lat.shape, lat.dtype)
    two, rows, cols = kv.shape
    vmem = pl.BlockSpec(memory_space=pltpu.VMEM)
    smem = pl.BlockSpec(memory_space=pltpu.SMEM)
    anyp = pl.BlockSpec(memory_space=pl.ANY)
    return pl.pallas_call(
        gather_kernel,
        in_specs=[smem, smem, vmem, anyp],
        out_specs=[vmem, vmem, anyp],
        out_shape=[block, block, jax.ShapeDtypeStruct((two, 2, rows // 2, cols), kv.dtype)],
        scratch_shapes=[pltpu.VMEM((4,) + lat.shape, lat.dtype), pltpu.VMEM(lat.shape, lat.dtype),
                        pltpu.VMEM((4,) + lat.shape, lat.dtype),
                        pltpu.SemaphoreType.DMA((7,)), pltpu.SemaphoreType.DMA((7,)),
                        pltpu.SemaphoreType.DMA],
        compiler_params=pltpu.CompilerParams(
            collective_id=0, has_side_effects=True, vmem_limit_bytes=58 * 1024 * 1024),
        cost_estimate=pl.CostEstimate(flops=0, bytes_accessed=20000000, transcendentals=0),
        name="gather",
    )(ancestors, order, lat, kv)


def choose(own, others, z, edge, need, c):
    at, row = need // 2, need % 2
    which = jnp.where(at == z, 0, jnp.where(at == 3 - z, 1, jnp.where(at == edge, 2, 3)))
    res = own[c, row]
    for i in range(3):
        res = jnp.where(which == i + 1, others(i, c, row), res)
    return res


def routed_kernel(anc_ref, ord_ref, own_ref, x0_ref, x1_ref, ew_ref, eb_ref, sh_ref, sc_ref,
                  gain_ref, w_ref, q_ref, k_ref, v_ref, others_ref, keys_ref,
                  normed, got_keys, got_vals, outward, landed, send, recv, *, chunk, width):
    g, me, s = lax.axis_index("groups"), lax.axis_index("particle"), lax.axis_index("seq")
    step = pl.program_id(0)
    last = pl.num_programs(0) - 1
    z, y = me // 2, me % 2
    inner = jnp.logical_or(z == 1, z == 2)
    outer = jnp.logical_not(inner)
    edge = jnp.where(z < 2, 0, 3)
    beside = jnp.where(z == 0, 1, jnp.where(z == 1, 0, jnp.where(z == 2, 3, 2)))

    def at(plane):
        return (g, 2 * plane + y, s)

    targets = (3 - z, beside, 3 - beside)

    def plane_copy(kind, c):
        return pltpu.make_async_remote_copy(
            src_ref=own_ref.at[c], dst_ref=(got_keys, got_vals)[c].at[kind], send_sem=send.at[2 * kind + c],
            recv_sem=recv.at[2 * kind + c], device_id=at(targets[kind]), device_id_type=MESH)

    key_copy = pltpu.make_async_remote_copy(
        src_ref=outward, dst_ref=landed, send_sem=send.at[6], recv_sem=recv.at[6],
        device_id=at(beside), device_id_type=MESH)

    @pl.when(step == 0)
    def _():
        greet([at((z + k) % 4) for k in (1, 2, 3)])

        @pl.when(inner)
        def _():
            for c in range(2):
                plane_copy(0, c).start()

        @pl.when(outer)
        def _():
            for c in range(2):
                plane_copy(2, c).start()
                plane_copy(1, c).start()

    @pl.when(jnp.logical_and(step == last, inner))
    def _():
        for kind in range(3):
            plane_copy(kind, 0).wait_recv()
        for i in range(2):
            outward[i] = choose(
                own_ref, lambda i, c, row: got_keys[i, row], z, edge, anc_ref[ord_ref[2 * edge + i]], 0)
        key_copy.start()

    project_kernel(x0_ref, x1_ref, ew_ref, eb_ref, sh_ref, sc_ref, gain_ref, w_ref,
                   q_ref, k_ref, v_ref, normed, chunk=chunk, width=width)

    @pl.when(step == last)
    def _():
        @pl.when(inner)
        def _():
            for kind in range(3):
                plane_copy(kind, 1).wait_recv()
            others_ref[:, 0] = got_keys[...]
            others_ref[:, 1] = got_vals[...]
            for c in range(2):
                plane_copy(0, c).wait_send()
            key_copy.wait_send()

        @pl.when(outer)
        def _():
            for c in range(2):
                plane_copy(2, c).wait_send()
                plane_copy(1, c).wait_send()
            key_copy.wait_recv()
            keys_ref[...] = landed[...]


def image_kernel(anc_ref, ord_ref, own_ref, others_ref, keys_ref, q_ref, k_ref, v_ref,
                 acc_ref, sum_ref, mine_ref, theirs_ref,
                 outward, landed, give, came, send, recv, *, chunk, unit):
    g, me, s = lax.axis_index("groups"), lax.axis_index("particle"), lax.axis_index("seq")
    step = pl.program_id(0)
    z, y = me // 2, me % 2
    inner = jnp.logical_or(z == 1, z == 2)
    edge = jnp.where(z < 2, 0, 3)
    beside = jnp.where(z == 0, 1, jnp.where(z == 1, 0, jnp.where(z == 2, 3, 2)))
    across = (g, 2 * z + 1 - y, s)
    along = (g, 2 * beside + y, s)

    out_copy = pltpu.make_async_remote_copy(
        src_ref=outward, dst_ref=landed, send_sem=send.at[0], recv_sem=recv.at[0],
        device_id=along, device_id_type=MESH)

    def swap_copy(c):
        return pltpu.make_async_remote_copy(
            src_ref=give.at[c], dst_ref=came.at[c], send_sem=send.at[1 + c],
            recv_sem=recv.at[1 + c], device_id=across, device_id_type=MESH)

    def find(c, need):
        return choose(own_ref, lambda i, c, row: others_ref[i, c, row], z, edge, need, c)

    need_mine = anc_ref[ord_ref[me]]
    need_give = anc_ref[ord_ref[2 * z + 1 - y]]

    def finish(c, far):
        for ref, need, slot in ((mine_ref, need_mine, y), (give, need_give, 1 - y)):
            ref[c] = jnp.where(need // 2 == z, own_ref[c, need % 2], far[slot])
        swap_copy(c).start()

    @pl.when(step == 0)
    def _():
        greet([across, along])

        @pl.when(inner)
        def _():
            for i in range(2):
                outward[i] = find(1, anc_ref[ord_ref[2 * edge + i]])
            out_copy.start()
            for c in range(2):
                mine_ref[c] = find(c, need_mine)
                give[c] = find(c, need_give)
                swap_copy(c).start()

        @pl.when(jnp.logical_not(inner))
        def _():
            finish(0, keys_ref)

    width = k_ref.shape[1]
    vals = jnp.concatenate([v_ref[...], jnp.ones_like(v_ref)], axis=1)
    for at in range(0, q_ref.shape[0], chunk):
        r = slice(at, at + chunk)
        sc = lax.dot_general(q_ref[r, :], k_ref[...], NT, preferred_element_type=F32)
        p = jnp.exp2(sc * unit).astype(BF16)
        o = jnp.dot(p, vals, preferred_element_type=F32)
        acc_ref[r, :] = o[:, :width]
        sum_ref[r, :] = o[:, width:]

    last = pl.num_programs(0) - 1

    @pl.when(jnp.logical_and(step == last - 1, jnp.logical_not(inner)))
    def _():
        out_copy.wait_recv()
        finish(1, landed)

    @pl.when(step == last)
    def _():
        @pl.when(inner)
        def _():
            out_copy.wait_send()

        for c in range(2):
            swap_copy(c).wait()
            theirs_ref[c] = came[c]


def image_attention(ancestors, order, own, others, keys, q, k, v, width):
    tokens, cols = q.shape
    heads = cols // width
    unit = LOG2E / width ** 0.5
    out = jax.ShapeDtypeStruct((tokens, cols), F32)
    two, _, rows, _ = own.shape
    text = jax.ShapeDtypeStruct((two, rows, cols), BF16)
    vmem = pl.BlockSpec(memory_space=pltpu.VMEM)
    smem = pl.BlockSpec(memory_space=pltpu.SMEM)
    head = pl.BlockSpec((tokens, width), lambda h: (0, h))
    return pl.pallas_call(
        functools.partial(image_kernel, chunk=256, unit=unit),
        grid=(heads,),
        in_specs=[smem, smem] + [vmem] * 3 + [head] * 3,
        out_specs=[head, head, vmem, vmem],
        out_shape=[out, out, text, text],
        scratch_shapes=[pltpu.VMEM(own.shape[1:], BF16), pltpu.VMEM(own.shape[1:], BF16),
                        pltpu.VMEM(text.shape, BF16), pltpu.VMEM(text.shape, BF16),
                        pltpu.SemaphoreType.DMA((3,)), pltpu.SemaphoreType.DMA((3,))],
        compiler_params=pltpu.CompilerParams(
            collective_id=1, has_side_effects=True, vmem_limit_bytes=58 * 1024 * 1024),
        cost_estimate=pl.CostEstimate(
            flops=8 * tokens * tokens * cols, bytes_accessed=14 * tokens * cols,
            transcendentals=tokens * tokens * heads),
        name="image",
    )(ancestors, order, own, others, keys, q, k, v)


def body(latents, text_kv, ancestors, order, embed_weight, embed_bias, shift, scale,
         qkv_weight, norm_gains, *, particles):
    width = norm_gains.shape[1]
    seq = lax.axis_index("seq")
    lat = pack(latents[0].astype(BF16))
    kv = text_kv[0]
    small = (embed_weight, embed_bias, shift, scale, norm_gains, qkv_weight)
    if particles == 8:
        x_other, x_mine, planes = gather(ancestors, order, lat, kv)
        q, k, v, others, keys = project(x_other, x_mine, *small, route=(ancestors, order, planes))
        acc, total, own, swapped = image_attention(
            ancestors, order, planes, others, keys, q, k, v, width)
        (ka, va), (kb, vb) = own, swapped
    else:
        need = ancestors[order][lax.axis_index("particle")]
        x_mine = lax.all_gather(lat, "particle", axis=0)[need]
        x_other = lax.ppermute(x_mine, "seq", [(0, 1), (1, 0)])
        text = lax.all_gather(kv, "particle", axis=0)[need]
        rows = text.shape[1] // 2
        ka, kb, va, vb = text[0, :rows], text[0, rows:], text[1, :rows], text[1, rows:]
        q, k, v = project(x_other, x_mine, *small)
        acc, total = image_alone(q, k, v, width)
    away = text_attention(q, ka, kb, va, vb, acc, total, 0, width)
    theirs = lax.ppermute(away, "seq", [(0, 1), (1, 0)])
    mine = text_attention(q, ka, kb, va, vb, acc, total, 1, width)
    left = jnp.where(seq == 0, mine, theirs)
    right = jnp.where(seq == 0, theirs, mine)
    return jnp.concatenate([left, right], axis=1)[None]


def solution(mesh):
    in_specs = (
        P(("groups", "particle"), "seq", None),
        P(("groups", "particle"), None, None, "seq"),
        P("groups"),
        P("groups"),
        P(),
        P(),
        P("groups"),
        P("groups"),
        P(None, "seq"),
        P(),
    )
    out_specs = P(("groups", "particle"), "seq", None)
    run = functools.partial(body, particles=mesh.shape["particle"])
    return jax.shard_map(run, mesh=mesh, in_specs=in_specs, out_specs=out_specs, check_vma=False)
```
